32 devices in a mesh: gx: 8 (over z, x), gy: 4 (over y, core).
Axes of the slice: x: 2, y: 2, z: 4, core: 2. Of those that a mesh axis runs over, the one named last changes fastest.
Arguments:
- factor_grads: bfloat16 [128, 196608], P(('gx', 'gy')), may hold values from -0.29882812 to 0.29882812
- latents: bfloat16 [128, 1024], P(('gx', 'gy')), may hold values from -6 to 6
- task_ids: int32 [128], P(('gx', 'gy')), may hold values from 0 to 127, each once
- offsets: int32 [160], replicated, may hold values from 0 to 196607, as said below
- target_scale: float32 [160], replicated, may hold values from 0.5 to 2
- momentum: float32 [1024, 196608], P(None, ('gx', 'gy')), may hold values from -6 to 6
Outputs:
- new_momentum: float32 [1024, 196608], P(None, ('gx', 'gy'))
- step: float32 [1024, 196608], P(None, ('gx', 'gy'))
The draws below stay inside these ranges and needn't reach their ends.
Inputs may be any that keep to these rules, and one draw needn't show every extreme that they name: `task_ids`: a permutation of 0 to 127. offsets[0] is 0 and offsets rise strictly.
All inputs are finite; a program needn't handle non-finite values.
Results may differ from the reference program's by a relative error of at most 0.0003.
Values may be sent and summed in bfloat16 or wider, within the bound.
No kernel may reach another device: no remote copies, remote signals or barrier semaphores. Data moves between devices by JAX's collectives and lax.ppermute only.
A program may use at most 192 MiB of HBM per device.

```python
import math
import jax
import jax.numpy as jnp
from jax import lax

L = 1024
OUT = 196608
TARGETS = 160
ITERS = 2
TASKS = 128


def draw_offsets(key, part):
    cut_points = jax.random.permutation(key, OUT - 1)[:TARGETS - 1] + 1
    cut_points = jnp.sort(cut_points.astype(jnp.int32))
    return jnp.concatenate([jnp.zeros((1,), jnp.int32), cut_points]).astype(jnp.int32)


def block_levels(key, dims, shards, low, high):
    def one(axis_at, blocks):
        draws = jax.random.uniform(jax.random.fold_in(jax.random.fold_in(key, 6), axis_at), (blocks,), jnp.float32, low / len(shards), high / len(shards))
        return jnp.repeat(jnp.exp(draws), dims[axis_at] // blocks).reshape((-1,) + (1,) * (len(dims) - axis_at - 1))

    factor_of = one(*shards[0])
    for cut in shards[1:]:
        factor_of = factor_of * one(*cut)
    return factor_of


def gaussian(stream_key, shape, spread, limit, cuts=(), kind=jnp.bfloat16):
    entries = jax.random.normal(stream_key, shape, jnp.float32) * spread
    if len(cuts) > 0:
        entries = block_levels(stream_key, shape, cuts, -0.22, 0.18) * entries
    return jnp.clip(entries, min=-limit, max=limit).astype(kind)


def setup_inputs(seed: int = 0) -> dict:
    key_list = jax.random.split(jax.random.key(seed), 7)
    return {
        "factor_grads": gaussian(key_list[0], (TASKS, OUT), 0.05, 0.29882812, ((0, 32),)),
        "latents": gaussian(key_list[1], (TASKS, L), 1.0, 6.0, ((0, 32),)),
        "task_ids": jax.random.permutation(key_list[2], TASKS).astype(jnp.int32),
        "offsets": draw_offsets(jax.random.fold_in(key_list[6], 71), 0),
        "target_scale": jnp.clip(jnp.exp(jax.random.uniform(key_list[4], (TARGETS,), jnp.float32, math.log(0.5), math.log(2.0))), 0.5, 2.0),
        "momentum": gaussian(key_list[5], (L, OUT), 1.0, 6.0, ((1, 32),), jnp.float32),
    }


MOMENTUM_DECAY = 0.95
EPSILON = 1e-07
NEWTON_A = 3.4445
NEWTON_B = -4.775
NEWTON_C = 2.0315

def reference(factor_grads, latents, task_ids, offsets, target_scale, momentum):
    task_latent = latents[task_ids]
    head_grad = jnp.dot(task_latent.T, factor_grads, preferred_element_type=jnp.float32)
    new_momentum = MOMENTUM_DECAY * momentum + head_grad
    blended = head_grad + MOMENTUM_DECAY * new_momentum
    frobenius = jnp.sqrt(jnp.sum(blended * blended))
    orthogonal = blended / (frobenius + EPSILON)
    for iteration in range(ITERS):
        gram_matrix = jnp.dot(orthogonal, orthogonal.T, precision=lax.Precision.HIGHEST)
        poly_matrix = NEWTON_B * gram_matrix + NEWTON_C * jnp.dot(gram_matrix, gram_matrix, precision=lax.Precision.HIGHEST)
        orthogonal = NEWTON_A * orthogonal + jnp.dot(poly_matrix, orthogonal, precision=lax.Precision.HIGHEST)
    column_index = jnp.arange(OUT, dtype=jnp.int32)
    target_index = (jnp.searchsorted(offsets, column_index, side='right') - 1).astype(jnp.int32)
    column_scale = target_scale[target_index]
    step = math.sqrt(OUT) * column_scale[None, :] * orthogonal
    return (new_momentum, step)
```

```python
import functools
import math

import jax
import jax.numpy as jnp
from jax import lax
from jax.experimental import pallas as pl
from jax.experimental.pallas import tpu as pltpu
from jax.sharding import PartitionSpec as P

MOMENTUM_DECAY = 0.95
EPSILON = 1e-07
NEWTON_A = 3.4445
NEWTON_B = -4.775
NEWTON_C = 2.0315

AXES = ("gx", "gy")
BLOCK = 256
LANES = 128
PIECES = 3
PIECES_AT = (1, 2)
SMALL = pl.CostEstimate(flops=1, bytes_accessed=1, transcendentals=0)
F32 = jnp.float32
BF16 = jnp.bfloat16


def dot(a, b):
    return jnp.dot(a, b, preferred_element_type=F32)


def dot_nt(a, b):
    return lax.dot_general(a, b, (((1,), (1,)), ((), ())), preferred_element_type=F32)


def swap(x, distance, count):
    return lax.ppermute(x, AXES, [(i, i ^ distance) for i in range(count)])


def upper_blocks(size):
    return [(i, j) for i in range(size) for j in range(i, size)]


def column_tile(columns, limit):
    return max(t for t in range(LANES, limit + 1, LANES) if columns % t == 0)


def with_ids(latents, task_ids):
    id_columns = jnp.stack([task_ids // 256, task_ids % 256], axis=1).astype(BF16)
    return jnp.concatenate([latents, jnp.pad(id_columns, ((0, 0), (0, LANES - 2)))], axis=1)


def chosen_latents(held, me, rows, width):
    tasks = held.shape[0]
    place = jnp.arange(tasks, dtype=jnp.int32)
    origin = ((place // rows) ^ me) * rows + place % rows
    held_ids = held[:, width].astype(jnp.int32) * 256 + held[:, width + 1].astype(jnp.int32)
    ids = jnp.sum(jnp.where(origin[None, :] == place[:, None], held_ids[None, :], 0), axis=1)
    chosen = (ids[:, None] == origin[None, :]).astype(BF16)
    return dot(chosen, held[:, :width]).astype(BF16)


def tie_kernel(x_ref, after_ref, out_ref):
    del x_ref, after_ref, out_ref


def tied(x, after):
    anywhere = pl.BlockSpec(memory_space=pl.ANY)
    return pl.pallas_call(
        tie_kernel,
        in_specs=[anywhere, anywhere],
        out_specs=anywhere,
        out_shape=jax.ShapeDtypeStruct(x.shape, x.dtype),
        input_output_aliases={0: 0},
        cost_estimate=SMALL,
        name="tie",
    )(x, after)


def summed(x):
    return jnp.sum(jnp.sum(x, axis=1, keepdims=True), axis=0, keepdims=True)


def gram_kernel(momentum_ref, rounded_ref, gram_ref, note_ref, squares_ref):
    step = pl.program_id(0)

    @pl.when(step == 0)
    def _():
        gram_ref[...] = jnp.zeros_like(gram_ref)
        squares_ref[...] = jnp.zeros_like(squares_ref)

    momentum = momentum_ref[...]
    size, tile = momentum.shape
    squares_ref[...] += jnp.sum((momentum * momentum).reshape(size // 8, 8, tile), axis=0)
    rounded = momentum.astype(BF16)
    rounded_ref[...] = rounded
    for at, (i, j) in enumerate(upper_blocks(size // BLOCK)):
        gram_ref[at * BLOCK : (at + 1) * BLOCK, :] += dot_nt(
            rounded[i * BLOCK : (i + 1) * BLOCK], rounded[j * BLOCK : (j + 1) * BLOCK]
        )

    @pl.when(step == pl.num_programs(0) - 1)
    def _():
        note_ref[...] = jnp.broadcast_to(summed(squares_ref[...]), note_ref.shape)


def gram_pass(momentum):
    size, count = momentum.shape
    tile = column_tile(count, 1024)
    packed = len(upper_blocks(size // BLOCK)) * BLOCK
    return pl.pallas_call(
        gram_kernel,
        grid=(count // tile,),
        in_specs=[pl.BlockSpec((size, tile), lambda i: (0, i))],
        out_specs=[
            pl.BlockSpec((size, tile), lambda i: (0, i)),
            pl.BlockSpec((packed, BLOCK), lambda i: (0, 0)),
            pl.BlockSpec((8, LANES), lambda i: (0, 0)),
        ],
        out_shape=[
            jax.ShapeDtypeStruct((size, count), BF16),
            jax.ShapeDtypeStruct((packed, BLOCK), F32),
            jax.ShapeDtypeStruct((8, LANES), F32),
        ],
        scratch_shapes=[pltpu.VMEM((8, tile), F32)],
        compiler_params=pltpu.CompilerParams(vmem_limit_bytes=56 * 2**20),
        cost_estimate=SMALL,
        name="momentum_gram",
    )(momentum)


def cross_kernel(columns_ref, rounded_ref, cross_ref):
    size = rounded_ref.shape[0]

    @pl.when(pl.program_id(0) == 0)
    def _():
        cross_ref[...] = jnp.zeros_like(cross_ref)

    columns = columns_ref[...]
    cross_ref[:, :size] += dot_nt(columns, rounded_ref[...])
    cross_ref[:, size:] += dot_nt(columns, columns)


def cross_pass(columns, rounded):
    size, count = rounded.shape
    tasks = columns.shape[0]
    tile = column_tile(count, 2048)
    return pl.pallas_call(
        cross_kernel,
        grid=(count // tile,),
        in_specs=[
            pl.BlockSpec((tasks, tile), lambda i: (0, i)),
            pl.BlockSpec((size, tile), lambda i: (0, i)),
        ],
        out_specs=pl.BlockSpec((tasks, size + tasks), lambda i: (0, 0)),
        out_shape=jax.ShapeDtypeStruct((tasks, size + tasks), F32),
        compiler_params=pltpu.CompilerParams(vmem_limit_bytes=60 * 2**20),
        cost_estimate=pl.CostEstimate(
            flops=2 * size * tasks * count, bytes_accessed=2 * size * count, transcendentals=0
        ),
        name="cross_terms",
    )(columns, rounded)


def parted(x):
    high = x.astype(BF16)
    return high, (x - high.astype(F32)).astype(BF16)


def blended_kernel(side_ref, cross_ref, latent_ref, momentum_gram_ref, squares_ref, kept_ref, sent_ref, note_ref, gram_ref):
    tasks, size = latent_ref.shape
    alpha, beta = MOMENTUM_DECAY**2, 1.0 + MOMENTUM_DECAY
    latent = latent_ref[...]
    turned = latent.astype(F32).T.astype(BF16)
    twice = jnp.concatenate([latent, latent], axis=0)
    shares = jnp.concatenate(parted(cross_ref[:, size:]), axis=1)
    mixed = alpha * beta * cross_ref[:, :size] + 0.5 * beta * beta * dot(shares, twice)
    right = jnp.concatenate([twice, *parted(mixed)], axis=0)
    left = jnp.concatenate([*parted(mixed.T), turned, turned], axis=1)
    for at, (i, j) in enumerate(upper_blocks(size // BLOCK)):
        block = slice(at * BLOCK, (at + 1) * BLOCK)
        gram_ref[block, :] = alpha * alpha * momentum_gram_ref[block, :] + dot(
            left[i * BLOCK : (i + 1) * BLOCK, :], right[:, j * BLOCK : (j + 1) * BLOCK]
        )
    half = kept_ref.shape[0]
    side = side_ref[0]
    kept_ref[...] = gram_ref[pl.ds(pl.multiple_of(side * half, half), half), :]
    sent_ref[...] = gram_ref[pl.ds(pl.multiple_of((1 - side) * half, half), half), :].astype(BF16)

    total = alpha * alpha * squares_ref[0:1, 0:1] + 2.0 * summed(mixed * latent.astype(F32))
    total = jnp.broadcast_to(total, note_ref.shape)
    high = total.astype(BF16).astype(F32)
    middle = (total - high).astype(BF16).astype(F32)
    lane = lax.broadcasted_iota(jnp.int32, note_ref.shape, 1)
    note = jnp.where(
        lane == 0, high, jnp.where(lane == 1, middle, jnp.where(lane == 2, total - high - middle, 0.0))
    )
    note_ref[...] = note.astype(BF16)


def blended_gram(side, cross, latent, gram, squares):
    half = gram.shape[0] // 2
    whole = pl.BlockSpec(memory_space=pltpu.VMEM)
    return pl.pallas_call(
        blended_kernel,
        in_specs=[pl.BlockSpec(memory_space=pltpu.SMEM), whole, whole, whole, whole],
        out_specs=[whole, whole, whole],
        out_shape=[
            jax.ShapeDtypeStruct((half, BLOCK), F32),
            jax.ShapeDtypeStruct((half, BLOCK), BF16),
            jax.ShapeDtypeStruct((16, BLOCK), BF16),
        ],
        scratch_shapes=[pltpu.VMEM(gram.shape, F32)],
        compiler_params=pltpu.CompilerParams(vmem_limit_bytes=40 * 2**20),
        cost_estimate=pl.CostEstimate(
            flops=4 * latent.shape[0] * latent.shape[1] ** 2, bytes_accessed=8 * gram.size, transcendentals=0
        ),
        name="blended_gram",
    )(side, cross, latent, gram, squares)


def momentum_kernel(latent_ref, momentum_ref, columns_ref, *refs):
    new_ref, mark_ref = refs[-2:]
    head_grad = lax.dot_general(
        latent_ref[...], columns_ref[...], (((0,), (0,)), ((), ())), preferred_element_type=F32
    )
    new_ref[...] = MOMENTUM_DECAY * momentum_ref[...] + head_grad
    mark_ref[...] = jnp.zeros_like(mark_ref)


def momentum_piece(latent, momentum, columns, after, held, piece, pieces):
    size, count = momentum.shape
    tasks = columns.shape[0]
    tile = column_tile(count // pieces, 1024)
    steps = count // pieces // tile
    first = piece * steps
    anywhere = pl.BlockSpec(memory_space=pl.ANY)
    operands = (latent, momentum, columns, after) + (() if held is None else (held,))
    return pl.pallas_call(
        momentum_kernel,
        grid=(steps,),
        in_specs=[
            pl.BlockSpec((tasks, size), lambda i: (0, 0)),
            pl.BlockSpec((size, tile), lambda i: (0, i + first)),
            pl.BlockSpec((tasks, tile), lambda i: (0, i + first)),
        ]
        + [anywhere] * (len(operands) - 3),
        out_specs=[
            pl.BlockSpec((size, tile), lambda i: (0, i + first)),
            pl.BlockSpec((8, LANES), lambda i: (0, 0)),
        ],
        out_shape=[
            jax.ShapeDtypeStruct((size, count), F32),
            jax.ShapeDtypeStruct((8, LANES), F32),
        ],
        input_output_aliases={} if held is None else {4: 0},
        compiler_params=pltpu.CompilerParams(vmem_limit_bytes=56 * 2**20),
        cost_estimate=SMALL,
        name="new_momentum",
    )(*operands)


def poly_kernel(notes_ref, gram_ref, latent_ref, weight_ref, inverse_ref, x_ref, xb_ref, p_ref, pb_ref, d_ref):
    size = x_ref.shape[0]
    tasks = latent_ref.shape[0]
    blocks = size // BLOCK
    a, b, c = NEWTON_A, NEWTON_B, NEWTON_C
    beta = 1.0 + MOMENTUM_DECAY

    def part(i):
        return slice(i * BLOCK, (i + 1) * BLOCK)

    turned = latent_ref[...].astype(F32).T.astype(BF16)
    norm = jnp.sqrt(jnp.maximum(summed(notes_ref[...].astype(F32)), 0.0)) + EPSILON
    inverse_ref[...] = jnp.broadcast_to(1.0 / norm, inverse_ref.shape)
    inverse = 1.0 / (norm * norm)

    for at, (i, j) in enumerate(upper_blocks(blocks)):
        block = gram_ref[part(at), :].astype(F32) * inverse
        x_ref[part(i), part(j)] = block
        xb_ref[part(i), part(j)] = block.astype(BF16)
        if i != j:
            x_ref[part(j), part(i)] = block.T
            xb_ref[part(j), part(i)] = block.T.astype(BF16)
    for j in range(blocks):
        poly = b * x_ref[:, part(j)] + c * dot(xb_ref[...], xb_ref[:, part(j)])
        p_ref[:, part(j)] = poly
        pb_ref[:, part(j)] = poly.astype(BF16)
    for j in range(blocks):
        d_ref[:, part(j)] = (
            2 * a * p_ref[:, part(j)] + dot(pb_ref[...], pb_ref[:, part(j)])
        ).astype(BF16)
    for j in range(blocks):
        x_ref[:, part(j)] = a * a * x_ref[:, part(j)] + dot(xb_ref[...], d_ref[:, part(j)])
    xb_ref[...] = x_ref[...].astype(BF16)
    for j in range(blocks):
        poly = b * x_ref[:, part(j)] + c * dot(xb_ref[...], xb_ref[:, part(j)])
        p_ref[:, part(j)] = p_ref[:, part(j)] + poly
        d_ref[:, part(j)] = poly.astype(BF16)
    for j in range(blocks):
        rest = a * p_ref[:, part(j)] + dot(d_ref[...], pb_ref[:, part(j)])
        xb_ref[:, part(j)] = rest.astype(BF16)
        weight_ref[:, part(j)] = (MOMENTUM_DECAY**2 * rest).astype(BF16)
    side = beta * (a * a * turned.astype(F32) + dot(xb_ref[...], turned))
    high = side.astype(BF16)
    weight_ref[:, size : size + tasks] = high
    weight_ref[:, size + tasks :] = (side - high.astype(F32)).astype(BF16)


def poly_pass(notes, gram, latent):
    tasks, size = latent.shape
    whole = pl.BlockSpec(memory_space=pltpu.VMEM)
    return pl.pallas_call(
        poly_kernel,
        in_specs=[whole, whole, whole],
        out_specs=[whole, whole],
        out_shape=[
            jax.ShapeDtypeStruct((size, size + 2 * tasks), BF16),
            jax.ShapeDtypeStruct((8, LANES), F32),
        ],
        scratch_shapes=[
            pltpu.VMEM((size, size), F32),
            pltpu.VMEM((size, size), BF16),
            pltpu.VMEM((size, size), F32),
            pltpu.VMEM((size, size), BF16),
            pltpu.VMEM((size, size), BF16),
        ],
        compiler_params=pltpu.CompilerParams(vmem_limit_bytes=50 * 2**20),
        cost_estimate=pl.CostEstimate(flops=10 * size**3, bytes_accessed=4 * size * size, transcendentals=0),
        name="polynomial",
    )(notes, gram, latent)


def step_kernel(weight_ref, inverse_ref, scale_ref, momentum_ref, columns_ref, step_ref, right_ref):
    momentum = momentum_ref[...]
    size = momentum.shape[0]
    tasks = columns_ref.shape[0]
    right_ref[:size, :] = momentum.astype(BF16)
    right_ref[size : size + tasks, :] = columns_ref[...]
    right_ref[size + tasks :, :] = columns_ref[...]
    factor = NEWTON_A**2 * MOMENTUM_DECAY**2
    scale = scale_ref[...] * inverse_ref[0:1, 0:1]
    step_ref[...] = scale * (factor * momentum + dot(weight_ref[...], right_ref[...]))


def step_pass(weight, inverse, scale, momentum, columns):
    size, count = momentum.shape
    tasks = columns.shape[0]
    depth = weight.shape[1]
    tile = column_tile(count, 1024)
    return pl.pallas_call(
        step_kernel,
        grid=(count // tile,),
        in_specs=[
            pl.BlockSpec((size, depth), lambda i: (0, 0)),
            pl.BlockSpec((8, LANES), lambda i: (0, 0)),
            pl.BlockSpec((1, tile), lambda i: (0, i)),
            pl.BlockSpec((size, tile), lambda i: (0, i)),
            pl.BlockSpec((tasks, tile), lambda i: (0, i)),
        ],
        out_specs=pl.BlockSpec((size, tile), lambda i: (0, i)),
        out_shape=jax.ShapeDtypeStruct((size, count), F32),
        scratch_shapes=[pltpu.VMEM((depth, tile), BF16)],
        compiler_params=pltpu.CompilerParams(vmem_limit_bytes=50 * 2**20),
        cost_estimate=pl.CostEstimate(
            flops=2 * count * size * depth, bytes_accessed=8 * size * count, transcendentals=0
        ),
        name="step",
    )(weight, inverse, scale, momentum, columns)


def halves(gram, distance, me):
    half = gram.shape[0] // 2
    side = (me // distance) % 2
    sent = lax.dynamic_slice_in_dim(gram, (1 - side) * half, half, 0).astype(BF16)
    return lax.dynamic_slice_in_dim(gram, side * half, half, 0), sent


def doubled(gram, got, distance, me):
    side = (me // distance) % 2
    return jnp.concatenate(
        [jnp.where(side == 0, gram, got), jnp.where(side == 0, got, gram)], axis=0
    )


def per_device(out_total, factor_grads, latents, task_ids, offsets, target_scale, momentum):
    count = lax.axis_size(AXES)
    me = lax.axis_index(AXES)
    rows, size = latents.shape
    column_count = momentum.shape[1]
    distances = [2**k for k in range(count.bit_length() - 1)]

    columns = lax.all_to_all(factor_grads, AXES, split_axis=1, concat_axis=0, tiled=True)
    held = with_ids(latents, task_ids)
    rounded, gram, squares = gram_pass(momentum)
    cross = cross_pass(columns, rounded)
    for place, distance in enumerate(distances):
        got = swap(held, distance, count)
        if place == len(distances) - 2:
            got = tied(got, squares)
        if place == len(distances) - 1:
            got = tied(got, cross)
        held = jnp.concatenate([held, got], axis=0)
    latent = chosen_latents(held, me, rows, size)
    side = me % 2
    kept, sent, note = blended_gram(side.astype(jnp.int32).reshape(1), cross, latent, gram, squares)

    new_momentum = None
    for place, distance in enumerate(distances):
        if place > 0:
            kept, sent = halves(gram, distance, me)
        got = swap(sent, distance, count)
        if place in PIECES_AT:
            new_momentum, mark = momentum_piece(
                latent, momentum, columns, sent, new_momentum, place - PIECES_AT[0], PIECES
            )
            got = tied(got, mark)
        gram = kept + got.astype(F32)
    shard = gram.shape[0]
    gram = jnp.concatenate([gram.astype(BF16), note], axis=0)
    for distance in distances[::-1]:
        got = swap(gram, distance, count)
        if distance == 2:
            new_momentum, mark = momentum_piece(
                latent, momentum, columns, gram, new_momentum, PIECES - 1, PIECES
            )
            got = tied(got, mark)
        if distance > 1:
            gram = doubled(gram, got, distance, me)
    apart = [x.reshape(count // 2, -1, BLOCK) for x in (gram, got)]
    notes = jnp.concatenate([x[:, shard] for x in apart], axis=0)
    gram, got = [x[:, :shard].reshape(-1, BLOCK) for x in apart]
    gram = doubled(gram, got, 1, me)

    weight, inverse = poly_pass(notes, gram, latent)

    column = me * column_count + jnp.arange(column_count, dtype=jnp.int32)
    after = jnp.concatenate([offsets[1:], jnp.full((1,), out_total, offsets.dtype)])
    inside = (column[None, :] >= offsets[:, None]) & (column[None, :] < after[:, None])
    column_scale = jnp.sum(jnp.where(inside, target_scale[:, None], 0.0), axis=0, keepdims=True)
    scale = column_scale * math.sqrt(out_total)
    step = step_pass(weight, inverse, scale, momentum, columns)
    return new_momentum, step


def solution(mesh):
    split = P(None, AXES)

    def whole(factor_grads, latents, task_ids, offsets, target_scale, momentum):
        return jax.shard_map(
            functools.partial(per_device, momentum.shape[1]),
            mesh=mesh,
            in_specs=(P(AXES, None), P(AXES, None), P(AXES), P(), P(), split),
            out_specs=(split, split),
            check_vma=False,
        )(factor_grads, latents, task_ids, offsets, target_scale, momentum)

    return whole
```

```python
import functools
import math

import jax
import jax.numpy as jnp
from jax import lax
from jax.experimental import pallas as pl
from jax.experimental.pallas import tpu as pltpu
from jax.sharding import PartitionSpec as P

MOMENTUM_DECAY = 0.95
EPSILON = 1e-07
NEWTON_A = 3.4445
NEWTON_B = -4.775
NEWTON_C = 2.0315

AXES = ("gx", "gy")
BLOCK = 256
LANES = 128
PIECES = 3
PIECES_AT = (1, 2)
SMALL = pl.CostEstimate(flops=1, bytes_accessed=1, transcendentals=0)
F32 = jnp.float32
BF16 = jnp.bfloat16


def dot(a, b):
    return jnp.dot(a, b, preferred_element_type=F32)


def dot_nt(a, b):
    return lax.dot_general(a, b, (((1,), (1,)), ((), ())), preferred_element_type=F32)


def swap(x, distance, count):
    return lax.ppermute(x, AXES, [(i, i ^ distance) for i in range(count)])


def upper_blocks(size):
    return [(i, j) for i in range(size) for j in range(i, size)]


def column_tile(columns, limit):
    return max(t for t in range(LANES, limit + 1, LANES) if columns % t == 0)


def with_ids(latents, task_ids):
    id_columns = jnp.stack([task_ids // 256, task_ids % 256], axis=1).astype(BF16)
    return jnp.concatenate([latents, jnp.pad(id_columns, ((0, 0), (0, LANES - 2)))], axis=1)


def entire(x):
    return pl.BlockSpec(x.shape, lambda i: (0, 0))


def summed(x):
    return jnp.sum(jnp.sum(x, axis=1, keepdims=True), axis=0, keepdims=True)


def gram_kernel(momentum_ref, rounded_ref, gram_ref, note_ref, squares_ref):
    step = pl.program_id(0)

    @pl.when(step == 0)
    def _():
        gram_ref[...] = jnp.zeros_like(gram_ref)
        squares_ref[...] = jnp.zeros_like(squares_ref)

    momentum = momentum_ref[...]
    size, tile = momentum.shape
    squares_ref[...] += jnp.sum((momentum * momentum).reshape(size // 8, 8, tile), axis=0)
    rounded = momentum.astype(BF16)
    rounded_ref[...] = rounded
    for at, (i, j) in enumerate(upper_blocks(size // BLOCK)):
        gram_ref[at * BLOCK : (at + 1) * BLOCK, :] += dot_nt(
            rounded[i * BLOCK : (i + 1) * BLOCK], rounded[j * BLOCK : (j + 1) * BLOCK]
        )

    @pl.when(step == pl.num_programs(0) - 1)
    def _():
        note_ref[...] = jnp.broadcast_to(summed(squares_ref[...]), note_ref.shape)


def gram_pass(momentum):
    size, count = momentum.shape
    tile = column_tile(count, 1024)
    packed = len(upper_blocks(size // BLOCK)) * BLOCK
    return pl.pallas_call(
        gram_kernel,
        grid=(count // tile,),
        in_specs=[pl.BlockSpec((size, tile), lambda i: (0, i))],
        out_specs=[
            pl.BlockSpec((size, tile), lambda i: (0, i)),
            pl.BlockSpec((packed, BLOCK), lambda i: (0, 0)),
            pl.BlockSpec((8, LANES), lambda i: (0, 0)),
        ],
        out_shape=[
            jax.ShapeDtypeStruct((size, count), BF16),
            jax.ShapeDtypeStruct((packed, BLOCK), F32),
            jax.ShapeDtypeStruct((8, LANES), F32),
        ],
        scratch_shapes=[pltpu.VMEM((8, tile), F32)],
        compiler_params=pltpu.CompilerParams(vmem_limit_bytes=56 * 2**20),
        cost_estimate=SMALL,
        name="momentum_gram",
    )(momentum)


def cross_kernel(columns_ref, rounded_ref, cross_ref):
    size = rounded_ref.shape[0]

    @pl.when(pl.program_id(0) == 0)
    def _():
        cross_ref[...] = jnp.zeros_like(cross_ref)

    columns = columns_ref[...]
    cross_ref[:, :size] += dot_nt(columns, rounded_ref[...])
    cross_ref[:, size:] += dot_nt(columns, columns)


def cross_pass(columns, rounded):
    size, count = rounded.shape
    tasks = columns.shape[0]
    tile = column_tile(count, 2048)
    return pl.pallas_call(
        cross_kernel,
        grid=(count // tile,),
        in_specs=[
            pl.BlockSpec((tasks, tile), lambda i: (0, i)),
            pl.BlockSpec((size, tile), lambda i: (0, i)),
        ],
        out_specs=pl.BlockSpec((tasks, size + tasks), lambda i: (0, 0)),
        out_shape=jax.ShapeDtypeStruct((tasks, size + tasks), F32),
        compiler_params=pltpu.CompilerParams(vmem_limit_bytes=60 * 2**20),
        cost_estimate=pl.CostEstimate(
            flops=2 * size * tasks * count, bytes_accessed=2 * size * count, transcendentals=0
        ),
        name="cross_terms",
    )(columns, rounded)


def parted(x):
    high = x.astype(BF16)
    return high, (x - high.astype(F32)).astype(BF16)


def blended_kernel(side_ref, origin_ref, cross_ref, momentum_gram_ref, squares_ref, *refs):
    held_refs, (latent_ref, kept_ref, sent_ref, note_ref, gram_ref) = refs[:-5], refs[-5:]
    tasks, size = latent_ref.shape
    held = jnp.concatenate([ref[...] for ref in held_refs], axis=0)
    origin = jnp.broadcast_to(origin_ref[...], (tasks, tasks))
    lane = lax.broadcasted_iota(jnp.int32, (tasks, LANES), 1)
    digits = held[:, size:].astype(F32) * jnp.where(lane == 0, 256.0, jnp.where(lane == 1, 1.0, 0.0))
    row = lax.broadcasted_iota(jnp.int32, (tasks, tasks), 1).astype(F32)
    ids = jnp.where(origin == row, jnp.sum(digits, axis=1, keepdims=True), 0.0)
    chosen = (origin == jnp.sum(ids, axis=0, keepdims=True)).astype(F32).astype(BF16)
    latent_ref[...] = lax.dot_general(
        chosen, held[:, :size], (((0,), (0,)), ((), ())), preferred_element_type=F32
    ).astype(BF16)
    alpha, beta = MOMENTUM_DECAY**2, 1.0 + MOMENTUM_DECAY
    latent = latent_ref[...]
    turned = latent.astype(F32).T.astype(BF16)
    twice = jnp.concatenate([latent, latent], axis=0)
    shares = jnp.concatenate(parted(cross_ref[:, size:]), axis=1)
    mixed = alpha * beta * cross_ref[:, :size] + 0.5 * beta * beta * dot(shares, twice)
    right = jnp.concatenate([twice, *parted(mixed)], axis=0)
    left = jnp.concatenate([*parted(mixed.T), turned, turned], axis=1)
    for at, (i, j) in enumerate(upper_blocks(size // BLOCK)):
        block = slice(at * BLOCK, (at + 1) * BLOCK)
        gram_ref[block, :] = alpha * alpha * momentum_gram_ref[block, :] + dot(
            left[i * BLOCK : (i + 1) * BLOCK, :], right[:, j * BLOCK : (j + 1) * BLOCK]
        )
    half = kept_ref.shape[0]
    side = side_ref[0]
    kept_ref[...] = gram_ref[pl.ds(pl.multiple_of(side * half, half), half), :]
    sent_ref[...] = gram_ref[pl.ds(pl.multiple_of((1 - side) * half, half), half), :].astype(BF16)

    total = alpha * alpha * squares_ref[0:1, 0:1] + 2.0 * summed(mixed * latent.astype(F32))
    total = jnp.broadcast_to(total, note_ref.shape)
    high = total.astype(BF16).astype(F32)
    middle = (total - high).astype(BF16).astype(F32)
    lane = lax.broadcasted_iota(jnp.int32, note_ref.shape, 1)
    note = jnp.where(
        lane == 0, high, jnp.where(lane == 1, middle, jnp.where(lane == 2, total - high - middle, 0.0))
    )
    note_ref[...] = note.astype(BF16)


def blended_gram(side, origin, cross, gram, squares, held):
    half = gram.shape[0] // 2
    tasks, size = origin.shape[0], held[0].shape[1] - LANES
    operands = (origin, cross, gram, squares, *held)
    results = [
        jax.ShapeDtypeStruct((tasks, size), BF16),
        jax.ShapeDtypeStruct((half, BLOCK), F32),
        jax.ShapeDtypeStruct((half, BLOCK), BF16),
        jax.ShapeDtypeStruct((16, BLOCK), BF16),
    ]
    return pl.pallas_call(
        blended_kernel,
        grid=(1,),
        in_specs=[pl.BlockSpec(memory_space=pltpu.SMEM)] + [entire(x) for x in operands],
        out_specs=[entire(x) for x in results],
        out_shape=results,
        scratch_shapes=[pltpu.VMEM(gram.shape, F32)],
        compiler_params=pltpu.CompilerParams(vmem_limit_bytes=63 * 2**20),
        cost_estimate=pl.CostEstimate(flops=4 * tasks * size**2, bytes_accessed=8 * gram.size, transcendentals=0),
        name="blended_gram",
    )(side, *operands)


def momentum_kernel(latent_ref, momentum_ref, columns_ref, *refs):
    new_ref, mark_ref = refs[-2:]
    head_grad = lax.dot_general(
        latent_ref[...], columns_ref[...], (((0,), (0,)), ((), ())), preferred_element_type=F32
    )
    new_ref[...] = MOMENTUM_DECAY * momentum_ref[...] + head_grad
    mark_ref[...] = jnp.zeros_like(mark_ref)


def momentum_piece(latent, momentum, columns, after, held, piece, pieces):
    size, count = momentum.shape
    tasks = columns.shape[0]
    tile = column_tile(count // pieces, 1024)
    steps = count // pieces // tile
    first = piece * steps
    anywhere = pl.BlockSpec(memory_space=pl.ANY)
    operands = (latent, momentum, columns, after) + (() if held is None else (held,))
    return pl.pallas_call(
        momentum_kernel,
        grid=(steps,),
        in_specs=[
            pl.BlockSpec((tasks, size), lambda i: (0, 0)),
            pl.BlockSpec((size, tile), lambda i: (0, i + first)),
            pl.BlockSpec((tasks, tile), lambda i: (0, i + first)),
        ]
        + [anywhere] * (len(operands) - 3),
        out_specs=[
            pl.BlockSpec((size, tile), lambda i: (0, i + first)),
            pl.BlockSpec((1, BLOCK), lambda i: (0, 0)),
        ],
        out_shape=[
            jax.ShapeDtypeStruct((size, count), F32),
            jax.ShapeDtypeStruct((1, BLOCK), F32),
        ],
        input_output_aliases={} if held is None else {4: 0},
        compiler_params=pltpu.CompilerParams(vmem_limit_bytes=56 * 2**20),
        cost_estimate=SMALL,
        name="new_momentum",
    )(*operands)


def poly_kernel(notes_ref, scale_ref, gram_ref, latent_ref, weight_ref, factor_ref, x_ref, xb_ref, p_ref, pb_ref, d_ref, g_ref):
    size = x_ref.shape[0]
    tasks = latent_ref.shape[0]
    blocks = size // BLOCK
    a, b, c = NEWTON_A, NEWTON_B, NEWTON_C
    beta = 1.0 + MOMENTUM_DECAY

    def part(i):
        return slice(i * BLOCK, (i + 1) * BLOCK)

    turned = latent_ref[...].astype(F32).T.astype(BF16)
    norm = jnp.sqrt(jnp.maximum(summed(notes_ref[...].astype(F32)), 0.0)) + EPSILON
    whole = a * a * MOMENTUM_DECAY**2
    factor_ref[...] = scale_ref[...] * (whole / norm)
    inverse = 1.0 / (norm * norm)

    def product(left_ref, right_ref, j):
        return dot(left_ref[: (j + 1) * BLOCK, :], right_ref[:, part(j)])

    def spread(ref, j, value):
        ref[: (j + 1) * BLOCK, part(j)] = value.astype(BF16)
        for i in range(j):
            ref[part(j), part(i)] = value[part(i), :].T.astype(BF16)

    for at, (i, j) in enumerate(upper_blocks(blocks)):
        block = gram_ref[part(at), :].astype(F32) * inverse
        x_ref[part(i), part(j)] = block
        xb_ref[part(i), part(j)] = block.astype(BF16)
        if i != j:
            xb_ref[part(j), part(i)] = block.T.astype(BF16)
    upper = [(j, slice(0, (j + 1) * BLOCK)) for j in range(blocks)]
    for j, rows in upper:
        poly = b * x_ref[rows, part(j)] + c * product(xb_ref, xb_ref, j)
        p_ref[rows, part(j)] = poly
        spread(pb_ref, j, poly)
    for j, rows in upper:
        spread(d_ref, j, 2 * a * p_ref[rows, part(j)] + product(pb_ref, pb_ref, j))
    for j, rows in upper:
        gram = a * a * x_ref[rows, part(j)] + product(xb_ref, d_ref, j)
        x_ref[rows, part(j)] = gram
        spread(g_ref, j, gram)
    for j, rows in upper:
        poly = b * x_ref[rows, part(j)] + c * product(g_ref, g_ref, j)
        p_ref[rows, part(j)] = p_ref[rows, part(j)] + poly
        spread(d_ref, j, poly)
    for j, rows in upper:
        rest = a * p_ref[rows, part(j)] + product(d_ref, pb_ref, j)
        spread(xb_ref, j, rest)
        spread(weight_ref, j, (MOMENTUM_DECAY**2 / whole) * rest)
    side = (beta / whole) * (a * a * turned.astype(F32) + dot(xb_ref[...], turned))
    high = side.astype(BF16)
    weight_ref[:, size : size + tasks] = high
    weight_ref[:, size + tasks :] = (side - high.astype(F32)).astype(BF16)


def poly_pass(notes, scale, gram, latent):
    tasks, size = latent.shape
    operands = (notes, scale, gram, latent)
    results = [
        jax.ShapeDtypeStruct((size, size + 2 * tasks), BF16),
        jax.ShapeDtypeStruct(scale.shape, F32),
    ]
    return pl.pallas_call(
        poly_kernel,
        grid=(1,),
        in_specs=[entire(x) for x in operands],
        out_specs=[entire(x) for x in results],
        out_shape=results,
        scratch_shapes=[
            pltpu.VMEM((size, size), F32),
            pltpu.VMEM((size, size), BF16),
            pltpu.VMEM((size, size), F32),
            pltpu.VMEM((size, size), BF16),
            pltpu.VMEM((size, size), BF16),
            pltpu.VMEM((size, size), BF16),
        ],
        compiler_params=pltpu.CompilerParams(vmem_limit_bytes=50 * 2**20),
        cost_estimate=pl.CostEstimate(flops=10 * size**3, bytes_accessed=4 * size * size, transcendentals=0),
        name="polynomial",
    )(*operands)


def step_kernel(weight_ref, factor_ref, momentum_ref, columns_ref, step_ref, right_ref):
    momentum = momentum_ref[...]
    size = momentum.shape[0]
    tasks = columns_ref.shape[0]
    right_ref[:size, :] = momentum.astype(BF16)
    right_ref[size : size + tasks, :] = columns_ref[...]
    right_ref[size + tasks :, :] = columns_ref[...]
    step_ref[...] = factor_ref[...] * (momentum + dot(weight_ref[...], right_ref[...]))


def step_pass(weight, factor, momentum, columns):
    size, count = momentum.shape
    tasks = columns.shape[0]
    depth = weight.shape[1]
    tile = column_tile(count, 1024)
    return pl.pallas_call(
        step_kernel,
        grid=(count // tile,),
        in_specs=[
            pl.BlockSpec((size, depth), lambda i: (0, 0)),
            pl.BlockSpec((1, tile), lambda i: (0, i)),
            pl.BlockSpec((size, tile), lambda i: (0, i)),
            pl.BlockSpec((tasks, tile), lambda i: (0, i)),
        ],
        out_specs=pl.BlockSpec((size, tile), lambda i: (0, i)),
        out_shape=jax.ShapeDtypeStruct((size, count), F32),
        scratch_shapes=[pltpu.VMEM((depth, tile), BF16)],
        compiler_params=pltpu.CompilerParams(vmem_limit_bytes=50 * 2**20),
        cost_estimate=pl.CostEstimate(
            flops=2 * count * size * depth, bytes_accessed=8 * size * count, transcendentals=0
        ),
        name="step",
    )(weight, factor, momentum, columns)


def halves(gram, distance, me):
    half = gram.shape[0] // 2
    side = (me // distance) % 2
    sent = lax.dynamic_slice_in_dim(gram, (1 - side) * half, half, 0).astype(BF16)
    return lax.dynamic_slice_in_dim(gram, side * half, half, 0), sent


def doubled(gram, got, distance, me):
    side = (me // distance) % 2
    return jnp.concatenate(
        [jnp.where(side == 0, gram, got), jnp.where(side == 0, got, gram)], axis=0
    )


def per_device(out_total, factor_grads, latents, task_ids, offsets, target_scale, momentum):
    count = lax.axis_size(AXES)
    me = lax.axis_index(AXES)
    rows, size = latents.shape
    column_count = momentum.shape[1]
    distances = [2**k for k in range(count.bit_length() - 1)]

    columns = lax.all_to_all(factor_grads, AXES, split_axis=1, concat_axis=0, tiled=True)
    held = with_ids(latents, task_ids)
    rounded, gram, squares = gram_pass(momentum)
    cross = cross_pass(columns, rounded)
    for distance in distances[:-2]:
        held = jnp.concatenate([held, swap(held, distance, count)], axis=0)
    quarter = count // 4
    far = [swap(held, k * quarter, count) for k in (1, 2, 3)]
    place = jnp.arange(rows * count, dtype=jnp.int32)
    origin = (((place // rows) ^ me) * rows + place % rows).astype(F32).reshape(-1, 1)
    side = (me % 2).astype(jnp.int32).reshape(1)
    latent, kept, sent, note = blended_gram(side, origin, cross, gram, squares, [held] + far)

    new_momentum = None
    for place, distance in enumerate(distances):
        if place > 0:
            kept, sent = halves(gram, distance, me)
        got = swap(sent, distance, count)
        if place in PIECES_AT:
            new_momentum, mark = momentum_piece(
                latent, momentum, columns, sent, new_momentum, place - PIECES_AT[0], PIECES
            )
            kept = kept + mark
        gram = kept + got.astype(F32)
    shard = gram.shape[0]
    gram = jnp.concatenate([gram.astype(BF16), note], axis=0)
    for distance in distances[::-1]:
        got = swap(gram, distance, count)
        if distance == 2:
            new_momentum, mark = momentum_piece(
                latent, momentum, columns, gram, new_momentum, PIECES - 1, PIECES
            )
            got = got + mark.astype(BF16)
        if distance > 1:
            gram = doubled(gram, got, distance, me)
    apart = [x.reshape(count // 2, -1, BLOCK) for x in (gram, got)]
    notes = jnp.concatenate([x[:, shard] for x in apart], axis=0)
    gram, got = [x[:, :shard].reshape(-1, BLOCK) for x in apart]
    gram = doubled(gram, got, 1, me)

    column = me * column_count + jnp.arange(column_count, dtype=jnp.int32)
    after = jnp.concatenate([offsets[1:], jnp.full((1,), out_total, offsets.dtype)])
    inside = (column[None, :] >= offsets[:, None]) & (column[None, :] < after[:, None])
    column_scale = jnp.sum(jnp.where(inside, target_scale[:, None], 0.0), axis=0, keepdims=True)
    scale = column_scale * math.sqrt(out_total)
    weight, factor = poly_pass(notes, scale, gram, latent)
    step = step_pass(weight, factor, momentum, columns)
    return new_momentum, step


def solution(mesh):
    split = P(None, AXES)

    def whole(factor_grads, latents, task_ids, offsets, target_scale, momentum):
        return jax.shard_map(
            functools.partial(per_device, momentum.shape[1]),
            mesh=mesh,
            in_specs=(P(AXES, None), P(AXES, None), P(AXES), P(), P(), split),
            out_specs=(split, split),
            check_vma=False,
        )(factor_grads, latents, task_ids, offsets, target_scale, momentum)

    return whole
```

```python
import functools
import math

import jax
import jax.numpy as jnp
from jax import lax
from jax.experimental import pallas as pl
from jax.experimental.pallas import tpu as pltpu
from jax.sharding import PartitionSpec as P

MOMENTUM_DECAY = 0.95
EPSILON = 1e-07
NEWTON_A = 3.4445
NEWTON_B = -4.775
NEWTON_C = 2.0315

AXES = ("gx", "gy")
BLOCK = 256
LANES = 128
PIECES = (0, 2, 3, 4, 6)
SMALL = pl.CostEstimate(flops=1, bytes_accessed=1, transcendentals=0)
F32 = jnp.float32
BF16 = jnp.bfloat16


def dot(a, b):
    return jnp.dot(a, b, preferred_element_type=F32)


def dot_nt(a, b):
    return lax.dot_general(a, b, (((1,), (1,)), ((), ())), preferred_element_type=F32)


def swap(x, distance, count):
    return lax.ppermute(x, AXES, [(i, i ^ distance) for i in range(count)])


def upper_blocks(size):
    return [(i, j) for i in range(size) for j in range(i, size)]


def column_tile(columns, limit):
    return max(t for t in range(LANES, limit + 1, LANES) if columns % t == 0)


def with_ids(latents, task_ids):
    id_columns = jnp.stack([task_ids // 256, task_ids % 256], axis=1).astype(BF16)
    return jnp.concatenate([latents, jnp.pad(id_columns, ((0, 0), (0, LANES - 2)))], axis=1)


def entire(x):
    return pl.BlockSpec(x.shape, lambda i: (0, 0))


def summed(x):
    return jnp.sum(jnp.sum(x, axis=1, keepdims=True), axis=0, keepdims=True)


def gram_kernel(momentum_ref, rounded_ref, gram_ref, note_ref, squares_ref):
    step = pl.program_id(0)

    @pl.when(step == 0)
    def _():
        gram_ref[...] = jnp.zeros_like(gram_ref)
        squares_ref[...] = jnp.zeros_like(squares_ref)

    momentum = momentum_ref[...]
    size, tile = momentum.shape
    squares_ref[...] += jnp.sum((momentum * momentum).reshape(size // 8, 8, tile), axis=0)
    rounded = momentum.astype(BF16)
    rounded_ref[...] = rounded
    for at, (i, j) in enumerate(upper_blocks(size // BLOCK)):
        gram_ref[at * BLOCK : (at + 1) * BLOCK, :] += dot_nt(
            rounded[i * BLOCK : (i + 1) * BLOCK], rounded[j * BLOCK : (j + 1) * BLOCK]
        )

    @pl.when(step == pl.num_programs(0) - 1)
    def _():
        note_ref[...] = jnp.broadcast_to(summed(squares_ref[...]), note_ref.shape)


def gram_pass(momentum):
    size, count = momentum.shape
    tile = column_tile(count, 1024)
    packed = len(upper_blocks(size // BLOCK)) * BLOCK
    return pl.pallas_call(
        gram_kernel,
        grid=(count // tile,),
        in_specs=[pl.BlockSpec((size, tile), lambda i: (0, i))],
        out_specs=[
            pl.BlockSpec((size, tile), lambda i: (0, i)),
            pl.BlockSpec((packed, BLOCK), lambda i: (0, 0)),
            pl.BlockSpec((8, LANES), lambda i: (0, 0)),
        ],
        out_shape=[
            jax.ShapeDtypeStruct((size, count), BF16),
            jax.ShapeDtypeStruct((packed, BLOCK), F32),
            jax.ShapeDtypeStruct((8, LANES), F32),
        ],
        scratch_shapes=[pltpu.VMEM((8, tile), F32)],
        compiler_params=pltpu.CompilerParams(vmem_limit_bytes=56 * 2**20),
        cost_estimate=SMALL,
        name="momentum_gram",
    )(momentum)


def cross_kernel(columns_ref, rounded_ref, cross_ref):
    size = rounded_ref.shape[0]

    @pl.when(pl.program_id(0) == 0)
    def _():
        cross_ref[...] = jnp.zeros_like(cross_ref)

    columns = columns_ref[...]
    cross_ref[:, :size] += dot_nt(columns, rounded_ref[...])
    cross_ref[:, size:] += dot_nt(columns, columns)


def cross_pass(columns, rounded):
    size, count = rounded.shape
    tasks = columns.shape[0]
    tile = column_tile(count, 2048)
    return pl.pallas_call(
        cross_kernel,
        grid=(count // tile,),
        in_specs=[
            pl.BlockSpec((tasks, tile), lambda i: (0, i)),
            pl.BlockSpec((size, tile), lambda i: (0, i)),
        ],
        out_specs=pl.BlockSpec((tasks, size + tasks), lambda i: (0, 0)),
        out_shape=jax.ShapeDtypeStruct((tasks, size + tasks), F32),
        compiler_params=pltpu.CompilerParams(vmem_limit_bytes=60 * 2**20),
        cost_estimate=pl.CostEstimate(
            flops=2 * size * tasks * count, bytes_accessed=2 * size * count, transcendentals=0
        ),
        name="cross_terms",
    )(columns, rounded)


def parted(x):
    high = x.astype(BF16)
    return high, (x - high.astype(F32)).astype(BF16)


def blended_kernel(side_ref, origin_ref, cross_ref, momentum_gram_ref, squares_ref, *refs):
    held_refs, (latent_ref, kept_ref, sent_ref, note_ref, gram_ref) = refs[:-5], refs[-5:]
    tasks, size = latent_ref.shape
    held = jnp.concatenate([ref[...] for ref in held_refs], axis=0)
    origin = jnp.broadcast_to(origin_ref[...], (tasks, tasks))
    lane = lax.broadcasted_iota(jnp.int32, (tasks, LANES), 1)
    digits = held[:, size:].astype(F32) * jnp.where(lane == 0, 256.0, jnp.where(lane == 1, 1.0, 0.0))
    row = lax.broadcasted_iota(jnp.int32, (tasks, tasks), 1).astype(F32)
    ids = jnp.where(origin == row, jnp.sum(digits, axis=1, keepdims=True), 0.0)
    chosen = (origin == jnp.sum(ids, axis=0, keepdims=True)).astype(F32).astype(BF16)
    latent_ref[...] = lax.dot_general(
        chosen, held[:, :size], (((0,), (0,)), ((), ())), preferred_element_type=F32
    ).astype(BF16)
    alpha, beta = MOMENTUM_DECAY**2, 1.0 + MOMENTUM_DECAY
    latent = latent_ref[...]
    turned = latent.astype(F32).T.astype(BF16)
    twice = jnp.concatenate([latent, latent], axis=0)
    shares = jnp.concatenate(parted(cross_ref[:, size:]), axis=1)
    mixed = alpha * beta * cross_ref[:, :size] + 0.5 * beta * beta * dot(shares, twice)
    right = jnp.concatenate([twice, *parted(mixed)], axis=0)
    left = jnp.concatenate([*parted(mixed.T), turned, turned], axis=1)
    for at, (i, j) in enumerate(upper_blocks(size // BLOCK)):
        block = slice(at * BLOCK, (at + 1) * BLOCK)
        gram_ref[block, :] = alpha * alpha * momentum_gram_ref[block, :] + dot(
            left[i * BLOCK : (i + 1) * BLOCK, :], right[:, j * BLOCK : (j + 1) * BLOCK]
        )
    half = kept_ref.shape[0]
    side = side_ref[0]
    kept_ref[...] = gram_ref[pl.ds(pl.multiple_of(side * half, half), half), :]
    sent_ref[...] = gram_ref[pl.ds(pl.multiple_of((1 - side) * half, half), half), :].astype(BF16)

    total = alpha * alpha * squares_ref[0:1, 0:1] + 2.0 * summed(mixed * latent.astype(F32))
    total = jnp.broadcast_to(total, note_ref.shape)
    high = total.astype(BF16).astype(F32)
    middle = (total - high).astype(BF16).astype(F32)
    lane = lax.broadcasted_iota(jnp.int32, note_ref.shape, 1)
    note = jnp.where(
        lane == 0, high, jnp.where(lane == 1, middle, jnp.where(lane == 2, total - high - middle, 0.0))
    )
    note_ref[...] = note.astype(BF16)


def blended_gram(side, origin, cross, gram, squares, held):
    half = gram.shape[0] // 2
    tasks, size = origin.shape[0], held[0].shape[1] - LANES
    operands = (origin, cross, gram, squares, *held)
    results = [
        jax.ShapeDtypeStruct((tasks, size), BF16),
        jax.ShapeDtypeStruct((half, BLOCK), F32),
        jax.ShapeDtypeStruct((half, BLOCK), BF16),
        jax.ShapeDtypeStruct((16, BLOCK), BF16),
    ]
    return pl.pallas_call(
        blended_kernel,
        grid=(1,),
        in_specs=[pl.BlockSpec(memory_space=pltpu.SMEM)] + [entire(x) for x in operands],
        out_specs=[entire(x) for x in results],
        out_shape=results,
        scratch_shapes=[pltpu.VMEM(gram.shape, F32)],
        compiler_params=pltpu.CompilerParams(vmem_limit_bytes=63 * 2**20),
        cost_estimate=pl.CostEstimate(flops=4 * tasks * size**2, bytes_accessed=8 * gram.size, transcendentals=0),
        name="blended_gram",
    )(side, *operands)


def momentum_kernel(latent_ref, momentum_ref, columns_ref, *refs):
    new_ref, mark_ref = refs[-2:]
    head_grad = lax.dot_general(
        latent_ref[...], columns_ref[...], (((0,), (0,)), ((), ())), preferred_element_type=F32
    )
    new_ref[...] = MOMENTUM_DECAY * momentum_ref[...] + head_grad
    mark_ref[...] = jnp.zeros_like(mark_ref)


def momentum_piece(latent, momentum, columns, after, held, piece):
    size, count = momentum.shape
    tasks = columns.shape[0]
    begin, end = [share * count // PIECES[-1] for share in PIECES[piece : piece + 2]]
    steps = 2
    tile = (end - begin) // steps
    first = begin // tile
    anywhere = pl.BlockSpec(memory_space=pl.ANY)
    operands = (latent, momentum, columns, after) + (() if held is None else (held,))
    return pl.pallas_call(
        momentum_kernel,
        grid=(steps,),
        in_specs=[
            pl.BlockSpec((tasks, size), lambda i: (0, 0)),
            pl.BlockSpec((size, tile), lambda i: (0, i + first)),
            pl.BlockSpec((tasks, tile), lambda i: (0, i + first)),
        ]
        + [anywhere] * (len(operands) - 3),
        out_specs=[
            pl.BlockSpec((size, tile), lambda i: (0, i + first)),
            pl.BlockSpec((1, BLOCK), lambda i: (0, 0)),
        ],
        out_shape=[
            jax.ShapeDtypeStruct((size, count), F32),
            jax.ShapeDtypeStruct((1, BLOCK), F32),
        ],
        input_output_aliases={} if held is None else {4: 0},
        compiler_params=pltpu.CompilerParams(vmem_limit_bytes=56 * 2**20),
        cost_estimate=SMALL,
        name="new_momentum",
    )(*operands)


def poly_kernel(notes_ref, scale_ref, gram_ref, latent_ref, weight_ref, factor_ref, x_ref, xb_ref, p_ref, pb_ref, d_ref, g_ref):
    size = x_ref.shape[0]
    tasks = latent_ref.shape[0]
    blocks = size // BLOCK
    a, b, c = NEWTON_A, NEWTON_B, NEWTON_C
    beta = 1.0 + MOMENTUM_DECAY

    def part(i):
        return slice(i * BLOCK, (i + 1) * BLOCK)

    turned = latent_ref[...].astype(F32).T.astype(BF16)
    norm = jnp.sqrt(jnp.maximum(summed(notes_ref[...].astype(F32)), 0.0)) + EPSILON
    whole = a * a * MOMENTUM_DECAY**2
    factor_ref[...] = scale_ref[...] * (whole / norm)
    inverse = 1.0 / (norm * norm)

    def product(left_ref, right_ref, j):
        return dot(left_ref[: (j + 1) * BLOCK, :], right_ref[:, part(j)])

    def spread(ref, j, value):
        ref[: (j + 1) * BLOCK, part(j)] = value.astype(BF16)
        for i in range(j):
            ref[part(j), part(i)] = value[part(i), :].T.astype(BF16)

    for at, (i, j) in enumerate(upper_blocks(blocks)):
        block = gram_ref[part(at), :].astype(F32) * inverse
        x_ref[part(i), part(j)] = block
        xb_ref[part(i), part(j)] = block.astype(BF16)
        if i != j:
            xb_ref[part(j), part(i)] = block.T.astype(BF16)
    upper = [(j, slice(0, (j + 1) * BLOCK)) for j in range(blocks)]
    for j, rows in upper:
        poly = b * x_ref[rows, part(j)] + c * product(xb_ref, xb_ref, j)
        p_ref[rows, part(j)] = poly
        spread(pb_ref, j, poly)
    for j, rows in upper:
        spread(d_ref, j, 2 * a * p_ref[rows, part(j)] + product(pb_ref, pb_ref, j))
    for j, rows in upper:
        gram = a * a * x_ref[rows, part(j)] + product(xb_ref, d_ref, j)
        x_ref[rows, part(j)] = gram
        spread(g_ref, j, gram)
    for j, rows in upper:
        poly = b * x_ref[rows, part(j)] + c * product(g_ref, g_ref, j)
        p_ref[rows, part(j)] = p_ref[rows, part(j)] + poly
        spread(d_ref, j, poly)
    for j, rows in upper:
        rest = a * p_ref[rows, part(j)] + product(d_ref, pb_ref, j)
        spread(weight_ref, j, (1.0 / (a * a)) * rest)
    side = (beta / MOMENTUM_DECAY**2) * (turned.astype(F32) + dot(weight_ref[:, :size], turned))
    high = side.astype(BF16)
    weight_ref[:, size : size + tasks] = high
    weight_ref[:, size + tasks :] = (side - high.astype(F32)).astype(BF16)


def poly_pass(notes, scale, gram, latent):
    tasks, size = latent.shape
    operands = (notes, scale, gram, latent)
    results = [
        jax.ShapeDtypeStruct((size, size + 2 * tasks), BF16),
        jax.ShapeDtypeStruct(scale.shape, F32),
    ]
    return pl.pallas_call(
        poly_kernel,
        grid=(1,),
        in_specs=[entire(x) for x in operands],
        out_specs=[entire(x) for x in results],
        out_shape=results,
        scratch_shapes=[
            pltpu.VMEM((size, size), F32),
            pltpu.VMEM((size, size), BF16),
            pltpu.VMEM((size, size), F32),
            pltpu.VMEM((size, size), BF16),
            pltpu.VMEM((size, size), BF16),
            pltpu.VMEM((size, size), BF16),
        ],
        compiler_params=pltpu.CompilerParams(vmem_limit_bytes=50 * 2**20),
        cost_estimate=pl.CostEstimate(flops=10 * size**3, bytes_accessed=4 * size * size, transcendentals=0),
        name="polynomial",
    )(*operands)


def step_kernel(weight_ref, factor_ref, momentum_ref, columns_ref, step_ref, right_ref):
    momentum = momentum_ref[...]
    size = momentum.shape[0]
    tasks = columns_ref.shape[0]
    right_ref[:size, :] = momentum.astype(BF16)
    right_ref[size : size + tasks, :] = columns_ref[...]
    right_ref[size + tasks :, :] = columns_ref[...]
    step_ref[...] = factor_ref[...] * (momentum + dot(weight_ref[...], right_ref[...]))


def step_pass(weight, factor, momentum, columns):
    size, count = momentum.shape
    tasks = columns.shape[0]
    depth = weight.shape[1]
    tile = column_tile(count, 1024)
    return pl.pallas_call(
        step_kernel,
        grid=(count // tile,),
        in_specs=[
            pl.BlockSpec((size, depth), lambda i: (0, 0)),
            pl.BlockSpec((1, tile), lambda i: (0, i)),
            pl.BlockSpec((size, tile), lambda i: (0, i)),
            pl.BlockSpec((tasks, tile), lambda i: (0, i)),
        ],
        out_specs=pl.BlockSpec((size, tile), lambda i: (0, i)),
        out_shape=jax.ShapeDtypeStruct((size, count), F32),
        scratch_shapes=[pltpu.VMEM((depth, tile), BF16)],
        compiler_params=pltpu.CompilerParams(vmem_limit_bytes=50 * 2**20),
        cost_estimate=pl.CostEstimate(
            flops=2 * count * size * depth, bytes_accessed=8 * size * count, transcendentals=0
        ),
        name="step",
    )(weight, factor, momentum, columns)


def halves(gram, distance, me):
    half = gram.shape[0] // 2
    side = (me // distance) % 2
    sent = lax.dynamic_slice_in_dim(gram, (1 - side) * half, half, 0).astype(BF16)
    return lax.dynamic_slice_in_dim(gram, side * half, half, 0), sent


def doubled(gram, got, distance, me):
    side = (me // distance) % 2
    return jnp.concatenate(
        [jnp.where(side == 0, gram, got), jnp.where(side == 0, got, gram)], axis=0
    )


def per_device(out_total, factor_grads, latents, task_ids, offsets, target_scale, momentum):
    count = lax.axis_size(AXES)
    me = lax.axis_index(AXES)
    rows, size = latents.shape
    column_count = momentum.shape[1]
    distances = [2**k for k in range(count.bit_length() - 1)]

    columns = lax.all_to_all(factor_grads, AXES, split_axis=1, concat_axis=0, tiled=True)
    held = with_ids(latents, task_ids)
    rounded, gram, squares = gram_pass(momentum)
    cross = cross_pass(columns, rounded)
    for distance in distances[:-2]:
        held = jnp.concatenate([held, swap(held, distance, count)], axis=0)
    quarter = count // 4
    far = [swap(held, k * quarter, count) for k in (1, 2, 3)]
    place = jnp.arange(rows * count, dtype=jnp.int32)
    origin = (((place // rows) ^ me) * rows + place % rows).astype(F32).reshape(-1, 1)
    side = (me % 2).astype(jnp.int32).reshape(1)
    latent, kept, sent, note = blended_gram(side, origin, cross, gram, squares, [held] + far)

    new_momentum = None
    for place, distance in enumerate(distances[:-1]):
        if place > 0:
            kept, sent = halves(gram, distance, me)
        got = swap(sent, distance, count)
        if place in (1, 2):
            new_momentum, mark = momentum_piece(
                latent, momentum, columns, sent, new_momentum, place - 1
            )
            kept = kept + mark
        gram = kept + got.astype(F32)
    shard = gram.shape[0]
    sent = jnp.concatenate([gram.astype(BF16), note], axis=0)
    got = swap(sent, distances[-1], count)
    gram = (sent[:shard].astype(F32) + got[:shard].astype(F32)).astype(BF16)
    row = lax.broadcasted_iota(jnp.int32, note.shape, 0)
    note = jnp.where(row == 0, note, jnp.where(row == 1, got[shard:], jnp.zeros_like(note)))
    gram = jnp.concatenate([gram, note], axis=0)
    for place, distance in reversed(list(enumerate(distances[:-1]))):
        got = swap(gram, distance, count)
        if place in (1, 2):
            new_momentum, mark = momentum_piece(
                latent, momentum, columns, gram, new_momentum, 4 - place
            )
            got = got + mark.astype(BF16)
        if place > 0:
            gram = doubled(gram, got, distance, me)
    apart = [x.reshape(count // 4, -1, BLOCK) for x in (gram, got)]
    notes = jnp.concatenate([x[:, shard : shard + 2].reshape(-1, BLOCK) for x in apart], axis=0)
    gram, got = [x[:, :shard].reshape(-1, BLOCK) for x in apart]
    gram = doubled(gram, got, 1, me)

    column = me * column_count + jnp.arange(column_count, dtype=jnp.int32)
    after = jnp.concatenate([offsets[1:], jnp.full((1,), out_total, offsets.dtype)])
    inside = (column[None, :] >= offsets[:, None]) & (column[None, :] < after[:, None])
    column_scale = jnp.sum(jnp.where(inside, target_scale[:, None], 0.0), axis=0, keepdims=True)
    scale = column_scale * math.sqrt(out_total)
    weight, factor = poly_pass(notes, scale, gram, latent)
    step = step_pass(weight, factor, momentum, columns)
    return new_momentum, step


def solution(mesh):
    split = P(None, AXES)

    def whole(factor_grads, latents, task_ids, offsets, target_scale, momentum):
        return jax.shard_map(
            functools.partial(per_device, momentum.shape[1]),
            mesh=mesh,
            in_specs=(P(AXES, None), P(AXES, None), P(AXES), P(), P(), split),
            out_specs=(split, split),
            check_vma=False,
        )(factor_grads, latents, task_ids, offsets, target_scale, momentum)

    return whole
```

```python
import functools
import math

import jax
import jax.numpy as jnp
from jax import lax
from jax.experimental import pallas as pl
from jax.experimental.pallas import tpu as pltpu
from jax.sharding import PartitionSpec as P

MOMENTUM_DECAY = 0.95
EPSILON = 1e-07
NEWTON_A = 3.4445
NEWTON_B = -4.775
NEWTON_C = 2.0315

AXES = ("gx", "gy")
BLOCK = 256
LANES = 128
PIECES = (0, 2, 3, 4, 6)
SMALL = pl.CostEstimate(flops=1, bytes_accessed=1, transcendentals=0)
F32 = jnp.float32
BF16 = jnp.bfloat16


def dot(a, b):
    return jnp.dot(a, b, preferred_element_type=F32)


def dot_nt(a, b):
    return lax.dot_general(a, b, (((1,), (1,)), ((), ())), preferred_element_type=F32)


def swap(x, distance, count):
    return lax.ppermute(x, AXES, [(i, i ^ distance) for i in range(count)])


def upper_blocks(size):
    return [(i, j) for i in range(size) for j in range(i, size)]


def column_tile(columns, limit):
    return max(t for t in range(LANES, limit + 1, LANES) if columns % t == 0)


def with_ids(latents, task_ids):
    id_columns = jnp.stack([task_ids // 256, task_ids % 256], axis=1).astype(BF16)
    return jnp.concatenate([latents, jnp.pad(id_columns, ((0, 0), (0, LANES - 2)))], axis=1)


def entire(x):
    return pl.BlockSpec(x.shape, lambda i: (0, 0))


def summed(x):
    return jnp.sum(jnp.sum(x, axis=1, keepdims=True), axis=0, keepdims=True)


def gram_kernel(momentum_ref, rounded_ref, gram_ref, note_ref, squares_ref):
    step = pl.program_id(0)

    @pl.when(step == 0)
    def _():
        gram_ref[...] = jnp.zeros_like(gram_ref)
        squares_ref[...] = jnp.zeros_like(squares_ref)

    momentum = momentum_ref[...]
    size, tile = momentum.shape
    squares_ref[...] += jnp.sum((momentum * momentum).reshape(size // 8, 8, tile), axis=0)
    rounded = momentum.astype(BF16)
    rounded_ref[...] = rounded
    for at, (i, j) in enumerate(upper_blocks(size // BLOCK)):
        gram_ref[at * BLOCK : (at + 1) * BLOCK, :] += dot_nt(
            rounded[i * BLOCK : (i + 1) * BLOCK], rounded[j * BLOCK : (j + 1) * BLOCK]
        )

    @pl.when(step == pl.num_programs(0) - 1)
    def _():
        note_ref[...] = jnp.broadcast_to(summed(squares_ref[...]), note_ref.shape)


def gram_pass(momentum):
    size, count = momentum.shape
    tile = column_tile(count, 1024)
    packed = len(upper_blocks(size // BLOCK)) * BLOCK
    return pl.pallas_call(
        gram_kernel,
        grid=(count // tile,),
        in_specs=[pl.BlockSpec((size, tile), lambda i: (0, i))],
        out_specs=[
            pl.BlockSpec((size, tile), lambda i: (0, i)),
            pl.BlockSpec((packed, BLOCK), lambda i: (0, 0)),
            pl.BlockSpec((8, LANES), lambda i: (0, 0)),
        ],
        out_shape=[
            jax.ShapeDtypeStruct((size, count), BF16),
            jax.ShapeDtypeStruct((packed, BLOCK), F32),
            jax.ShapeDtypeStruct((8, LANES), F32),
        ],
        scratch_shapes=[pltpu.VMEM((8, tile), F32)],
        compiler_params=pltpu.CompilerParams(vmem_limit_bytes=56 * 2**20),
        cost_estimate=SMALL,
        name="momentum_gram",
    )(momentum)


def cross_kernel(columns_ref, rounded_ref, cross_ref):
    size = rounded_ref.shape[0]

    @pl.when(pl.program_id(0) == 0)
    def _():
        cross_ref[...] = jnp.zeros_like(cross_ref)

    columns = columns_ref[...]
    cross_ref[:, :size] += dot_nt(columns, rounded_ref[...])
    cross_ref[:, size:] += dot_nt(columns, columns)


def cross_pass(columns, rounded):
    size, count = rounded.shape
    tasks = columns.shape[0]
    tile = column_tile(count, 3072)
    return pl.pallas_call(
        cross_kernel,
        grid=(count // tile,),
        in_specs=[
            pl.BlockSpec((tasks, tile), lambda i: (0, i)),
            pl.BlockSpec((size, tile), lambda i: (0, i)),
        ],
        out_specs=pl.BlockSpec((tasks, size + tasks), lambda i: (0, 0)),
        out_shape=jax.ShapeDtypeStruct((tasks, size + tasks), F32),
        compiler_params=pltpu.CompilerParams(vmem_limit_bytes=60 * 2**20),
        cost_estimate=pl.CostEstimate(
            flops=2 * size * tasks * count, bytes_accessed=2 * size * count, transcendentals=0
        ),
        name="cross_terms",
    )(columns, rounded)


def parted(x):
    high = x.astype(BF16)
    return high, (x - high.astype(F32)).astype(BF16)


def blended_kernel(side_ref, origin_ref, cross_ref, momentum_gram_ref, squares_ref, *refs):
    held_refs, (latent_ref, kept_ref, sent_ref, note_ref, gram_ref) = refs[:-5], refs[-5:]
    tasks, size = latent_ref.shape
    held = jnp.concatenate([ref[...] for ref in held_refs], axis=0)
    origin = jnp.broadcast_to(origin_ref[...], (tasks, tasks))
    lane = lax.broadcasted_iota(jnp.int32, (tasks, LANES), 1)
    digits = held[:, size:].astype(F32) * jnp.where(lane == 0, 256.0, jnp.where(lane == 1, 1.0, 0.0))
    row = lax.broadcasted_iota(jnp.int32, (tasks, tasks), 1).astype(F32)
    ids = jnp.where(origin == row, jnp.sum(digits, axis=1, keepdims=True), 0.0)
    chosen = (origin == jnp.sum(ids, axis=0, keepdims=True)).astype(F32).astype(BF16)
    latent_ref[...] = lax.dot_general(
        chosen, held[:, :size], (((0,), (0,)), ((), ())), preferred_element_type=F32
    ).astype(BF16)
    alpha, beta = MOMENTUM_DECAY**2, 1.0 + MOMENTUM_DECAY
    latent = latent_ref[...]
    turned = latent.astype(F32).T.astype(BF16)
    twice = jnp.concatenate([latent, latent], axis=0)
    shares = jnp.concatenate(parted(cross_ref[:, size:]), axis=1)
    mixed = alpha * beta * cross_ref[:, :size] + 0.5 * beta * beta * dot(shares, twice)
    right = jnp.concatenate([twice, *parted(mixed)], axis=0)
    left = jnp.concatenate([*parted(mixed.T), turned, turned], axis=1)
    for at, (i, j) in enumerate(upper_blocks(size // BLOCK)):
        block = slice(at * BLOCK, (at + 1) * BLOCK)
        gram_ref[block, :] = alpha * alpha * momentum_gram_ref[block, :] + dot(
            left[i * BLOCK : (i + 1) * BLOCK, :], right[:, j * BLOCK : (j + 1) * BLOCK]
        )
    half = kept_ref.shape[0]
    side = side_ref[0]
    kept_ref[...] = gram_ref[pl.ds(pl.multiple_of(side * half, half), half), :]
    sent_ref[...] = gram_ref[pl.ds(pl.multiple_of((1 - side) * half, half), half), :].astype(BF16)

    total = alpha * alpha * squares_ref[0:1, 0:1] + 2.0 * summed(mixed * latent.astype(F32))
    total = jnp.broadcast_to(total, note_ref.shape)
    high = total.astype(BF16).astype(F32)
    middle = (total - high).astype(BF16).astype(F32)
    lane = lax.broadcasted_iota(jnp.int32, note_ref.shape, 1)
    note = jnp.where(
        lane == 0, high, jnp.where(lane == 1, middle, jnp.where(lane == 2, total - high - middle, 0.0))
    )
    note_ref[...] = note.astype(BF16)


def blended_gram(side, origin, cross, gram, squares, held):
    half = gram.shape[0] // 2
    tasks, size = origin.shape[0], held[0].shape[1] - LANES
    operands = (origin, cross, gram, squares, *held)
    results = [
        jax.ShapeDtypeStruct((tasks, size), BF16),
        jax.ShapeDtypeStruct((half, BLOCK), F32),
        jax.ShapeDtypeStruct((half, BLOCK), BF16),
        jax.ShapeDtypeStruct((16, BLOCK), BF16),
    ]
    return pl.pallas_call(
        blended_kernel,
        grid=(1,),
        in_specs=[pl.BlockSpec(memory_space=pltpu.SMEM)] + [entire(x) for x in operands],
        out_specs=[entire(x) for x in results],
        out_shape=results,
        scratch_shapes=[pltpu.VMEM(gram.shape, F32)],
        compiler_params=pltpu.CompilerParams(vmem_limit_bytes=63 * 2**20),
        cost_estimate=pl.CostEstimate(flops=4 * tasks * size**2, bytes_accessed=8 * gram.size, transcendentals=0),
        name="blended_gram",
    )(side, *operands)


def momentum_kernel(latent_ref, momentum_ref, columns_ref, *refs):
    new_ref, mark_ref = refs[-2:]
    head_grad = lax.dot_general(
        latent_ref[...], columns_ref[...], (((0,), (0,)), ((), ())), preferred_element_type=F32
    )
    new_ref[...] = MOMENTUM_DECAY * momentum_ref[...] + head_grad
    mark_ref[...] = jnp.zeros_like(mark_ref)


def momentum_piece(latent, momentum, columns, after, held, piece):
    size, count = momentum.shape
    tasks = columns.shape[0]
    begin, end = [share * count // PIECES[-1] for share in PIECES[piece : piece + 2]]
    steps = 2
    tile = (end - begin) // steps
    first = begin // tile
    anywhere = pl.BlockSpec(memory_space=pl.ANY)
    operands = (latent, momentum, columns, after) + (() if held is None else (held,))
    return pl.pallas_call(
        momentum_kernel,
        grid=(steps,),
        in_specs=[
            pl.BlockSpec((tasks, size), lambda i: (0, 0)),
            pl.BlockSpec((size, tile), lambda i: (0, i + first)),
            pl.BlockSpec((tasks, tile), lambda i: (0, i + first)),
        ]
        + [anywhere] * (len(operands) - 3),
        out_specs=[
            pl.BlockSpec((size, tile), lambda i: (0, i + first)),
            pl.BlockSpec((1, BLOCK), lambda i: (0, 0)),
        ],
        out_shape=[
            jax.ShapeDtypeStruct((size, count), F32),
            jax.ShapeDtypeStruct((1, BLOCK), F32),
        ],
        input_output_aliases={} if held is None else {4: 0},
        compiler_params=pltpu.CompilerParams(vmem_limit_bytes=56 * 2**20),
        cost_estimate=SMALL,
        name="new_momentum",
    )(*operands)


def poly_kernel(notes_ref, scale_ref, gram_ref, latent_ref, weight_ref, factor_ref, x_ref, xb_ref, p_ref, pb_ref, d_ref, g_ref):
    size = x_ref.shape[0]
    tasks = latent_ref.shape[0]
    blocks = size // BLOCK
    a, b, c = NEWTON_A, NEWTON_B, NEWTON_C
    beta = 1.0 + MOMENTUM_DECAY

    def part(i):
        return slice(i * BLOCK, (i + 1) * BLOCK)

    turned = latent_ref[...].astype(F32).T.astype(BF16)
    norm = jnp.sqrt(jnp.maximum(summed(notes_ref[...].astype(F32)), 0.0)) + EPSILON
    whole = a * a * MOMENTUM_DECAY**2
    factor_ref[...] = scale_ref[...] * (whole / norm)
    inverse = 1.0 / (norm * norm)

    def product(left_ref, right_ref, j):
        return dot(left_ref[: (j + 1) * BLOCK, :], right_ref[:, part(j)])

    def spread(ref, j, value):
        ref[: (j + 1) * BLOCK, part(j)] = value.astype(BF16)
        for i in range(j):
            ref[part(j), part(i)] = value[part(i), :].T.astype(BF16)

    for at, (i, j) in enumerate(upper_blocks(blocks)):
        block = gram_ref[part(at), :].astype(F32) * inverse
        x_ref[part(i), part(j)] = block
        xb_ref[part(i), part(j)] = block.astype(BF16)
        if i != j:
            xb_ref[part(j), part(i)] = block.T.astype(BF16)
    upper = [(j, slice(0, (j + 1) * BLOCK)) for j in range(blocks)]
    for j, rows in upper:
        poly = b * x_ref[rows, part(j)] + c * product(xb_ref, xb_ref, j)
        p_ref[rows, part(j)] = poly
        spread(pb_ref, j, poly)
    for j, rows in upper:
        spread(d_ref, j, 2 * a * p_ref[rows, part(j)] + product(pb_ref, pb_ref, j))
    for j, rows in upper:
        gram = a * a * x_ref[rows, part(j)] + product(xb_ref, d_ref, j)
        x_ref[rows, part(j)] = gram
        spread(g_ref, j, gram)
    for j, rows in upper:
        poly = b * x_ref[rows, part(j)] + c * product(g_ref, g_ref, j)
        p_ref[rows, part(j)] = p_ref[rows, part(j)] + poly
        spread(d_ref, j, poly)
    for j, rows in upper:
        rest = a * p_ref[rows, part(j)] + product(d_ref, pb_ref, j)
        spread(weight_ref, j, (1.0 / (a * a)) * rest)
    side = (beta / MOMENTUM_DECAY**2) * (turned.astype(F32) + dot(weight_ref[:, :size], turned))
    high = side.astype(BF16)
    weight_ref[:, size : size + tasks] = high
    weight_ref[:, size + tasks :] = (side - high.astype(F32)).astype(BF16)


def poly_pass(notes, scale, gram, latent):
    tasks, size = latent.shape
    operands = (notes, scale, gram, latent)
    results = [
        jax.ShapeDtypeStruct((size, size + 2 * tasks), BF16),
        jax.ShapeDtypeStruct(scale.shape, F32),
    ]
    return pl.pallas_call(
        poly_kernel,
        grid=(1,),
        in_specs=[entire(x) for x in operands],
        out_specs=[entire(x) for x in results],
        out_shape=results,
        scratch_shapes=[
            pltpu.VMEM((size, size), F32),
            pltpu.VMEM((size, size), BF16),
            pltpu.VMEM((size, size), F32),
            pltpu.VMEM((size, size), BF16),
            pltpu.VMEM((size, size), BF16),
            pltpu.VMEM((size, size), BF16),
        ],
        compiler_params=pltpu.CompilerParams(vmem_limit_bytes=50 * 2**20),
        cost_estimate=pl.CostEstimate(flops=10 * size**3, bytes_accessed=4 * size * size, transcendentals=0),
        name="polynomial",
    )(*operands)


def step_kernel(weight_ref, factor_ref, momentum_ref, columns_ref, step_ref, right_ref):
    momentum = momentum_ref[...]
    size = momentum.shape[0]
    tasks = columns_ref.shape[0]
    right_ref[:size, :] = momentum.astype(BF16)
    right_ref[size : size + tasks, :] = columns_ref[...]
    right_ref[size + tasks :, :] = columns_ref[...]
    step_ref[...] = factor_ref[...] * (momentum + dot(weight_ref[...], right_ref[...]))


def step_pass(weight, factor, momentum, columns):
    size, count = momentum.shape
    tasks = columns.shape[0]
    depth = weight.shape[1]
    tile = column_tile(count, 1024)
    return pl.pallas_call(
        step_kernel,
        grid=(count // tile,),
        in_specs=[
            pl.BlockSpec((size, depth), lambda i: (0, 0)),
            pl.BlockSpec((1, tile), lambda i: (0, i)),
            pl.BlockSpec((size, tile), lambda i: (0, i)),
            pl.BlockSpec((tasks, tile), lambda i: (0, i)),
        ],
        out_specs=pl.BlockSpec((size, tile), lambda i: (0, i)),
        out_shape=jax.ShapeDtypeStruct((size, count), F32),
        scratch_shapes=[pltpu.VMEM((depth, tile), BF16)],
        compiler_params=pltpu.CompilerParams(vmem_limit_bytes=50 * 2**20),
        cost_estimate=pl.CostEstimate(
            flops=2 * count * size * depth, bytes_accessed=8 * size * count, transcendentals=0
        ),
        name="step",
    )(weight, factor, momentum, columns)


def halves(gram, distance, me):
    half = gram.shape[0] // 2
    side = (me // distance) % 2
    sent = lax.dynamic_slice_in_dim(gram, (1 - side) * half, half, 0).astype(BF16)
    return lax.dynamic_slice_in_dim(gram, side * half, half, 0), sent


def doubled(gram, got, distance, me):
    side = (me // distance) % 2
    return jnp.concatenate(
        [jnp.where(side == 0, gram, got), jnp.where(side == 0, got, gram)], axis=0
    )


def per_device(out_total, factor_grads, latents, task_ids, offsets, target_scale, momentum):
    count = lax.axis_size(AXES)
    me = lax.axis_index(AXES)
    rows, size = latents.shape
    column_count = momentum.shape[1]
    distances = [2**k for k in range(count.bit_length() - 1)]

    columns = lax.all_to_all(factor_grads, AXES, split_axis=1, concat_axis=0, tiled=True)
    held = with_ids(latents, task_ids)
    rounded, gram, squares = gram_pass(momentum)
    cross = cross_pass(columns, rounded)
    for distance in distances[:-2]:
        held = jnp.concatenate([held, swap(held, distance, count)], axis=0)
    quarter = count // 4
    far = [swap(held, k * quarter, count) for k in (1, 2, 3)]
    place = jnp.arange(rows * count, dtype=jnp.int32)
    origin = (((place // rows) ^ me) * rows + place % rows).astype(F32).reshape(-1, 1)
    side = (me % 2).astype(jnp.int32).reshape(1)
    latent, kept, sent, note = blended_gram(side, origin, cross, gram, squares, [held] + far)

    new_momentum = None
    for place, distance in enumerate(distances[:-1]):
        if place > 0:
            kept, sent = halves(gram, distance, me)
        got = swap(sent, distance, count)
        if place in (1, 2):
            new_momentum, mark = momentum_piece(
                latent, momentum, columns, sent, new_momentum, place - 1
            )
            kept = kept + mark
        gram = kept + got.astype(F32)
    shard = gram.shape[0]
    sent = jnp.concatenate([gram.astype(BF16), note], axis=0)
    got = swap(sent, distances[-1], count)
    gram = (sent[:shard].astype(F32) + got[:shard].astype(F32)).astype(BF16)
    row = lax.broadcasted_iota(jnp.int32, note.shape, 0)
    note = jnp.where(row == 0, note, jnp.where(row == 1, got[shard:], jnp.zeros_like(note)))
    gram = jnp.concatenate([gram, note], axis=0)
    for place, distance in reversed(list(enumerate(distances[:-1]))):
        got = swap(gram, distance, count)
        if place in (1, 2):
            new_momentum, mark = momentum_piece(
                latent, momentum, columns, gram, new_momentum, 4 - place
            )
            got = got + mark.astype(BF16)
        if place > 0:
            gram = doubled(gram, got, distance, me)
    apart = [x.reshape(count // 4, -1, BLOCK) for x in (gram, got)]
    notes = jnp.concatenate([x[:, shard : shard + 2].reshape(-1, BLOCK) for x in apart], axis=0)
    gram, got = [x[:, :shard].reshape(-1, BLOCK) for x in apart]
    gram = doubled(gram, got, 1, me)

    column = me * column_count + jnp.arange(column_count, dtype=jnp.int32)
    after = jnp.concatenate([offsets[1:], jnp.full((1,), out_total, offsets.dtype)])
    inside = (column[None, :] >= offsets[:, None]) & (column[None, :] < after[:, None])
    column_scale = jnp.sum(jnp.where(inside, target_scale[:, None], 0.0), axis=0, keepdims=True)
    scale = column_scale * math.sqrt(out_total)
    weight, factor = poly_pass(notes, scale, gram, latent)
    step = step_pass(weight, factor, momentum, columns)
    return new_momentum, step


def solution(mesh):
    split = P(None, AXES)

    def whole(factor_grads, latents, task_ids, offsets, target_scale, momentum):
        return jax.shard_map(
            functools.partial(per_device, momentum.shape[1]),
            mesh=mesh,
            in_specs=(P(AXES, None), P(AXES, None), P(AXES), P(), P(), split),
            out_specs=(split, split),
            check_vma=False,
        )(factor_grads, latents, task_ids, offsets, target_scale, momentum)

    return whole
```
